32 devices in a mesh: groups: 2 (over y), ep: 4 (over z), col: 4 (over x, core).
Axes of the slice: x: 2, y: 2, z: 4, core: 2. Of those that a mesh axis runs over, the one named last changes fastest.
Arguments:
- tokens: bfloat16 [128, 7168], P(('groups', 'ep')), parts along dimension 0, may hold values from -6 to 6
- routes: int32 [128, 8], P(('groups', 'ep')), parts along dimension 0, may hold values from 0 to 31, all different within a row; in each aligned block of 16 rows (0 to 15, 16 to 31, ...) at most 8 rows name the same one
- route_gates: float32 [128, 8], P(('groups', 'ep')), parts along dimension 0, may hold values from 0.05 to 1
- gate_weight: bfloat16 [32, 7168, 1024], P('ep', None, 'col'), may hold values from -0.0625 to 0.0625
- down_weight: bfloat16 [32, 1024, 7168], P('ep', 'col'), may hold values from -0.25 to 0.25
Outputs:
- mixed: bfloat16 [128, 7168], P(('groups', 'ep'), 'col'), parts along dimension 0
The draws below stay inside these ranges and needn't reach their ends.
There are 2 independent parts, one for each index of `groups`. The reference program is written for one: setup_inputs(seed, part) draws one part's arguments, and reference() takes and returns one part's arrays. A program takes and returns all parts, laid end to end along the dimension named above; an argument that names none is the same for every part. Nothing has to cross between parts.
Inputs may be any that keep to these rules, and one draw needn't show every extreme that they name: `routes`: each row names 8 different experts. In each aligned block of 16 rows no expert is named by more than 8 rows, a bound that some block reaches.
All inputs are finite; a program needn't handle non-finite values.
Results may differ from the reference program's by a relative error of at most 0.013.
Values may be sent and summed in bfloat16 or wider, within the bound.
A program may use at most 192 MiB of HBM per device.

```python
import math
import jax
import jax.numpy as jnp
import numpy as np
from jax import lax

D = 7168
HID = 1024
EXPERTS = 32
TOP = 8
TOK_EP = 16
CAP = 8
TOKENS = 64
N_COL = 4


def spiked(entries, own_key, source, target, blocks, factor):
    owner, partner = [(jnp.arange(entries.shape[position]) // (entries.shape[position] // blocks)).reshape([-1 if axis == position else 1 for axis in range(entries.ndim)]) for position in (source, target)]
    chosen = jax.random.permutation(own_key, blocks)[partner]
    strong = (owner == chosen) | (owner == (partner + blocks // 2) % blocks)
    return jnp.where(strong, factor * entries, entries)


def levels(key, extent, split, least, largest):
    def one(axis_at, parts):
        steps = jax.random.uniform(jax.random.fold_in(jax.random.fold_in(key, 6), axis_at), (parts,), jnp.float32, least / len(split), largest / len(split))
        return jnp.repeat(jnp.exp(steps), extent[axis_at] // parts).reshape((-1,) + (1,) * (len(extent) - axis_at - 1))

    gain = one(*split[0])
    for cut in split[1:]:
        gain = gain * one(*cut)
    return gain


def assign_block(stream_key, own, number, rows, number_of, top, limit, slope):
    sequence = jax.random.permutation(stream_key, number_of)
    heavy_load, usual = load_shares(number_of, rows * top, limit, slope, True), load_shares(number_of, rows * top, limit, slope, False)
    places = jnp.arange(number_of)

    def named(tallies, offset_by):
        used = int((tallies > 0).sum())
        fixed = max(1, used // 4)
        passed = fixed + (places - fixed + offset_by * (used - fixed)) % max(1, number_of - fixed)
        return jnp.zeros((number_of,), jnp.int32).at[sequence[jnp.where(places < fixed, places, passed)]].set(jnp.asarray(tallies, jnp.int32))

    tallies = jnp.where(number % 4 == 0, named(heavy_load, number // 4), named(usual, number - number // 4 - 1))
    mixed = jax.random.permutation(jax.random.fold_in(own, 3), number_of)
    donor, receiver = mixed[0:number_of // 2 * 2:2], mixed[1:number_of // 2 * 2:2]
    slack = jnp.minimum(tallies[donor] - 1, limit - tallies[receiver]) // 2
    slack = jnp.where((donor == sequence[0]) | (receiver == sequence[0]) | (tallies[receiver] == 0), 0, jnp.maximum(slack, 0))
    passed = jax.random.randint(jax.random.fold_in(own, 4), (number_of // 2,), 0, 1 << 20) % (slack + 1)
    tallies = tallies.at[donor].add(-passed).at[receiver].add(passed)
    labels = jnp.searchsorted(jnp.cumsum(tallies), jnp.arange(rows * top), side="right").astype(jnp.int32)
    table = labels.reshape(top, rows).T
    table = table[jax.random.permutation(jax.random.fold_in(own, 1), rows)]
    offset_by = jax.random.randint(jax.random.fold_in(own, 2), (rows, 1), 0, top)
    return jnp.take_along_axis(table, (jnp.arange(top)[None, :] + offset_by) % top, axis=1)


def load_shares(count, total, limit, skew, full):
    portions = [(1 << 20) // math.isqrt(rank ** skew) + 1 for rank in range(1, count + 1)]
    largest = limit if full else min(limit, max(-(-total // count), total * portions[0] // sum(portions)))
    least = 1 if total - largest >= count - 1 else 0
    holding, surplus = [largest] + [least] * (count - 1), total - largest - least * (count - 1)
    while surplus > 0:
        movable = [i for i in range(1, count) if holding[i] < largest] or [i for i in range(1, count) if holding[i] < limit]
        whole, remaining = sum([portions[i] for i in movable]), surplus
        for i in movable:
            addition = min(limit - holding[i], max(1, remaining * portions[i] // whole), surplus)
            holding[i] = holding[i] + addition
            surplus = surplus - addition
    return np.array(holding)


def noise(own_key, extent, width, reach, cuts=(), kind=jnp.bfloat16):
    result = jax.random.normal(own_key, extent, jnp.float32) * width
    if len(cuts) > 0:
        result = levels(own_key, extent, cuts, -0.22, 0.18) * result
    return jnp.clip(result, min=-reach, max=reach).astype(kind)


def noise_with(rng, extent, deviation, reach, cuts, heavy, held_as=jnp.bfloat16):
    values = deviation * jax.random.normal(rng, extent, jnp.float32)
    if cuts:
        values = values * levels(rng, extent, cuts, -0.22, 0.18)
    return jnp.clip(spiked(values, jax.random.fold_in(rng, 3), *heavy), -reach, reach).astype(held_as)


def setup_inputs(seed: int = 0, part: int = 0) -> dict:
    key_list = jax.random.split(jax.random.key(seed), 6)
    part_splits = jax.random.split(jax.random.fold_in(key_list[5], part), 6)
    tokens = noise(part_splits[0], (TOKENS, D), 1.0, 6.0, ((0, 4),))
    routes_keys = jax.random.split(jax.random.fold_in(part_splits[1], 1), TOKENS // TOK_EP)
    routes_turns = jax.random.permutation(jax.random.fold_in(part_splits[1], 3), TOKENS // TOK_EP)
    routes = jax.vmap(lambda own, number: assign_block(jax.random.fold_in(part_splits[1], 2), own, number, TOK_EP, EXPERTS, TOP, CAP, 2))(routes_keys, routes_turns).reshape((TOKENS, TOP))
    route_gates = jnp.clip(jnp.exp(math.log(1.0) - 2.9957323 * jax.random.uniform(part_splits[2], (TOKENS, TOP), jnp.float32) ** levels(part_splits[2], (TOKENS, TOP), ((0, 4),), -0.2, 0.2)), 0.05, 1.0)
    gate_weight = noise(key_list[3], (EXPERTS, D, HID), D ** -0.5, 0.0625, ((0, 4), (2, 4)))
    down_weight = noise_with(key_list[4], (EXPERTS, HID, D), HID ** -0.5, 0.25, ((0, 4), (1, 4)), (1, 2, 4, 2.0))
    return {"tokens": tokens, "routes": routes, "route_gates": route_gates, "gate_weight": gate_weight, "down_weight": down_weight}


def reference(tokens, routes, route_gates, gate_weight, down_weight):
    slice_width = HID // N_COL

    def one_expert(running, packed):
        expert_id, w_gate, w_down = packed
        hidden = jax.nn.silu(jnp.dot(tokens, w_gate, preferred_element_type=jnp.float32)).astype(jnp.bfloat16)
        hidden_parts = hidden.astype(jnp.float32).reshape(TOKENS, N_COL, slice_width)
        down_parts = w_down.astype(jnp.float32).reshape(N_COL, slice_width, D)
        partial_value = jnp.einsum('tch,chd->ctd', hidden_parts, down_parts).astype(jnp.bfloat16)
        summed = jnp.sum(partial_value.astype(jnp.float32), axis=0)
        weight = jnp.sum(jnp.where(routes == expert_id, route_gates, jnp.zeros_like(route_gates)), axis=1)
        return running + weight[:, None] * summed, None

    start = jnp.zeros((TOKENS, D), jnp.float32)
    expert_ids = jnp.arange(EXPERTS, dtype=jnp.int32)
    running, unused = lax.scan(one_expert, start, (expert_ids, gate_weight, down_weight))
    return running.astype(jnp.bfloat16)
```

```python
import functools

import jax
import jax.numpy as jnp
from jax import lax
from jax.experimental import pallas as pl
from jax.experimental.pallas import tpu as pltpu
from jax.sharding import PartitionSpec as P

MESH = pl.DeviceIdType.MESH
AHEAD = 2


def kernel(
    n_ep, n_col, width,
    tok_hbm, routes_ref, gates_ref, wg_hbm, wd_hbm, out_ref,
    tok_all, g_all, wg_buf, wd_buf, h_buf, part, sbuf, rbuf, zsend, zown, zrecv,
    tok_sem, wg_sem, wd_sem, tz_send, tz_recv, gz_send, gz_recv,
    tc_send, tc_recv, rc_send, rc_recv, rz_send, rz_recv,
):
    rows, depth = tok_hbm.shape
    quarter = depth // n_col
    local_experts, hid = wg_buf.shape[0], wg_buf.shape[2]
    chunks = wd_buf.shape[0]
    lanes = g_all.shape[1]
    total = tok_all.shape[0]
    bits = []
    while (1 << len(bits)) < n_col:
        bits.append(1 << len(bits))
    me = lax.axis_index("ep")
    col = lax.axis_index("col")

    def low(k):
        return k & -k if k else n_col

    def partner(bit):
        return col + bit - 2 * bit * lax.rem(lax.div(col, bit), 2)

    def piece(k):
        p = col
        for bit in bits:
            if k & bit:
                p = p + bit - 2 * bit * lax.rem(lax.div(col, bit), 2)
        return p

    def block(index):
        return pl.ds(pl.multiple_of(index * rows, rows), rows)

    def columns(k):
        return pl.ds(pl.multiple_of(piece(k) * quarter, 128), quarter)

    def wg_copy(e):
        return pltpu.make_async_copy(wg_hbm.at[e], wg_buf.at[e], wg_sem.at[e])

    def wd_copy(j, k):
        at = pl.ds(pl.multiple_of(piece(k) * quarter + j * width, 128), width)
        return pltpu.make_async_copy(
            wd_hbm.at[:, :, at], wd_buf.at[j, k], wd_sem.at[j, k]
        )

    def wd_start(j):
        for k in range(n_col):
            wd_copy(j, k).start()

    def tok_z(d):
        return pltpu.make_async_remote_copy(
            src_ref=tok_hbm.at[:, columns(0)],
            dst_ref=tok_all.at[block(me), columns(0)],
            send_sem=tz_send.at[d], recv_sem=tz_recv.at[d],
            device_id={"ep": lax.rem(me + d, n_ep)}, device_id_type=MESH,
        )

    def gate_z(d):
        return pltpu.make_async_remote_copy(
            src_ref=g_all.at[block(me)], dst_ref=g_all.at[block(me)],
            send_sem=gz_send.at[d], recv_sem=gz_recv.at[d],
            device_id={"ep": lax.rem(me + d, n_ep)}, device_id_type=MESH,
        )

    def tok_c(d, k, bit):
        view = tok_all.at[block(lax.rem(me - d + n_ep, n_ep)), columns(k)]
        return pltpu.make_async_remote_copy(
            src_ref=view, dst_ref=view,
            send_sem=tc_send.at[d, k | bit], recv_sem=tc_recv.at[d, k | bit],
            device_id={"col": partner(bit)}, device_id_type=MESH,
        )

    def red_c(j, k):
        return pltpu.make_async_remote_copy(
            src_ref=sbuf.at[j, k - 1], dst_ref=rbuf.at[j, k - 1],
            send_sem=rc_send.at[j, k], recv_sem=rc_recv.at[j, k],
            device_id={"col": partner(low(k))}, device_id_type=MESH,
        )

    def red_z(j, d):
        return pltpu.make_async_remote_copy(
            src_ref=zsend.at[j, lax.rem(me + d, n_ep)], dst_ref=zrecv.at[j, d - 1],
            send_sem=rz_send.at[j, d], recv_sem=rz_recv.at[j, d],
            device_id={"ep": lax.rem(me + d, n_ep)}, device_id_type=MESH,
        )

    def each(lo, hi, body):
        def step(i, carry):
            body(i)
            return carry
        lax.fori_loop(lo, hi, step, 0)

    own_copy = pltpu.make_async_copy(tok_hbm, tok_all.at[block(me)], tok_sem)
    own_copy.start()
    wg_copy(0).start()

    barrier = pltpu.get_barrier_semaphore()
    each(1, n_ep, lambda d: pl.semaphore_signal(
        barrier, inc=1, device_id={"ep": lax.rem(me + d, n_ep)}, device_id_type=MESH))
    for bit in bits:
        pl.semaphore_signal(
            barrier, inc=1, device_id={"col": partner(bit)}, device_id_type=MESH)

    expert = lax.broadcasted_iota(jnp.int32, (rows, lanes), 1)
    dense = jnp.zeros((rows, lanes), jnp.float32)
    for k in range(routes_ref.shape[1]):
        dense = dense + jnp.where(
            routes_ref[:, k : k + 1] == expert, gates_ref[:, k : k + 1], 0.0)
    g_all[block(me), :] = dense

    pl.semaphore_wait(barrier, n_ep - 1 + len(bits))

    each(1, n_ep, lambda d: tok_z(d).start())
    each(1, n_ep, lambda d: gate_z(d).start())
    each(1, local_experts, lambda e: wg_copy(e).start())
    each(0, min(AHEAD, chunks), wd_start)

    def arrived(d):
        tok_z(d).wait_recv()
        for bit in reversed(bits):
            tok_c(d, 0, bit).start()

    each(1, n_ep, arrived)
    for bit in reversed(bits):
        higher = [k for k in range(1, n_col) if low(k) == bit]

        def relay(d):
            for k in higher:
                tok_c(d, k ^ bit, bit).wait_recv()
                for b in reversed(bits):
                    if b < bit:
                        tok_c(d, k, b).start()

        each(1, n_ep, relay)
    each(1, n_ep, lambda d: gate_z(d).wait_recv())
    own_copy.wait()

    def up(e):
        wg_copy(e).wait()

        @pl.when(e + AHEAD < chunks)
        def _():
            wd_start(e + AHEAD)

        v = jnp.dot(tok_all[...], wg_buf[e], preferred_element_type=jnp.float32)
        mine = lax.broadcasted_iota(jnp.int32, (total, lanes), 1) == me * local_experts + e
        weight = jnp.sum(jnp.where(mine, g_all[...], 0.0), axis=1, keepdims=True)
        h = v / (1.0 + jnp.exp(-v))
        h_buf[:, pl.ds(pl.multiple_of(e * hid, 128), hid)] = (h * weight).astype(h_buf.dtype)

    each(0, local_experts, up)
    each(min(local_experts + AHEAD, chunks), chunks, wd_start)

    order = [k for k in range(n_col) if k & 1] + [k for k in range(n_col) if not k & 1]
    if n_col == 1:
        order = [0]

    def down(j):
        for k in order:
            wd_copy(j, k).wait()
            y = jnp.dot(
                h_buf[...], wd_buf[j, k].reshape(local_experts * hid, width),
                preferred_element_type=jnp.float32)
            if k & 1:
                sbuf[j, k - 1] = y.astype(sbuf.dtype)
                red_c(j, k).start()
            else:
                part[j, k // 2] = y

    def reduce_stage(j, bit):
        for k in reversed(range(0, n_col, 2 * bit)):
            red_c(j, k | bit).wait_recv()
            y = part[j, k // 2] + rbuf[j, (k | bit) - 1].astype(jnp.float32)
            if k and low(k) == 2 * bit:
                sbuf[j, k - 1] = y.astype(sbuf.dtype)
                red_c(j, k).start()
            elif k or 2 * bit < n_col:
                part[j, k // 2] = y
            else:
                finish(j, y)

    def finish(j, y):
        part[j, 0] = y
        zsend[j] = y.astype(zsend.dtype).reshape(n_ep, rows, width)
        zown[j] = part[j, 0, block(me), :]
        each(1, n_ep, lambda d: red_z(j, d).start())

    def step(t):
        @pl.when(t < chunks)
        def _():
            down(t)

        for i, bit in enumerate(bits):
            j = t - 1 - i

            @pl.when((j >= 0) & (j < chunks))
            def _():
                reduce_stage(j, bit)

    each(0, chunks + len(bits), step)

    def last(j):
        def add(d, y):
            red_z(j, d).wait_recv()
            return y + zrecv[j, d - 1].astype(jnp.float32)

        y = lax.fori_loop(1, n_ep, add, zown[j])
        out_ref[:, pl.ds(pl.multiple_of(j * width, 128), width)] = y.astype(out_ref.dtype)

    each(0, chunks, last)

    def sent(d):
        tok_z(d).wait_send()
        gate_z(d).wait_send()
        for k in range(1, n_col):
            tok_c(d, k ^ low(k), low(k)).wait_send()

    each(1, n_ep, sent)

    def sent_chunk(j):
        for k in range(1, n_col):
            red_c(j, k).wait_send()
        each(1, n_ep, lambda d: red_z(j, d).wait_send())

    each(0, chunks, sent_chunk)


def on_device(tokens, routes, route_gates, gate_weight, down_weight):
    rows, depth = tokens.shape
    local_experts, _, hid = gate_weight.shape
    n_ep, n_col = lax.axis_size("ep"), lax.axis_size("col")
    quarter = depth // n_col
    width = 256 if quarter % 256 == 0 else 128
    chunks = quarter // width
    total = n_ep * rows
    lanes = -(-local_experts * n_ep // 128) * 128
    bf16, f32 = jnp.bfloat16, jnp.float32
    dma = pltpu.SemaphoreType.DMA
    vmem = pl.BlockSpec(memory_space=pltpu.VMEM)
    hbm = pl.BlockSpec(memory_space=pl.ANY)
    flops = 4 * total * depth * local_experts * hid
    return pl.pallas_call(
        functools.partial(kernel, n_ep, n_col, width),
        out_shape=jax.ShapeDtypeStruct((rows, quarter), tokens.dtype),
        in_specs=[hbm, vmem, vmem, hbm, hbm],
        out_specs=vmem,
        scratch_shapes=[
            pltpu.VMEM((total, depth), bf16),
            pltpu.VMEM((total, lanes), f32),
            pltpu.VMEM((local_experts, depth, hid), bf16),
            pltpu.VMEM((chunks, n_col, local_experts, hid, width), bf16),
            pltpu.VMEM((total, local_experts * hid), bf16),
            pltpu.VMEM((chunks, max(1, n_col // 2), total, width), f32),
            pltpu.VMEM((chunks, n_col - 1, total, width), bf16),
            pltpu.VMEM((chunks, n_col - 1, total, width), bf16),
            pltpu.VMEM((chunks, n_ep, rows, width), bf16),
            pltpu.VMEM((chunks, rows, width), f32),
            pltpu.VMEM((chunks, n_ep - 1, rows, width), bf16),
            dma,
            dma((local_experts,)),
            dma((chunks, n_col)),
            dma((n_ep,)), dma((n_ep,)), dma((n_ep,)), dma((n_ep,)),
            dma((n_ep, n_col)), dma((n_ep, n_col)),
            dma((chunks, n_col)), dma((chunks, n_col)),
            dma((chunks, n_ep)), dma((chunks, n_ep)),
        ],
        compiler_params=pltpu.CompilerParams(
            collective_id=0, has_side_effects=True, vmem_limit_bytes=63 * 1024 * 1024
        ),
        cost_estimate=pl.CostEstimate(
            flops=flops, bytes_accessed=4 * local_experts * depth * hid, transcendentals=0
        ),
    )(tokens, routes, route_gates, gate_weight, down_weight)


def solution(mesh):
    in_specs = (
        P(("groups", "ep"), None),
        P(("groups", "ep"), None),
        P(("groups", "ep"), None),
        P("ep", None, "col"),
        P("ep", "col", None),
    )
    out_specs = P(("groups", "ep"), "col")
    return jax.shard_map(
        on_device, mesh=mesh, in_specs=in_specs, out_specs=out_specs, check_vma=False
    )
```

```python
import functools

import jax
import jax.numpy as jnp
from jax import lax
from jax.experimental import pallas as pl
from jax.experimental.pallas import tpu as pltpu
from jax.sharding import PartitionSpec as P

MESH = pl.DeviceIdType.MESH
AHEAD = 2
LAG = 2


def kernel(
    n_ep, n_col, width,
    tok_hbm, routes_ref, gates_ref, wg_hbm, wd_hbm, out_ref,
    tok_all, g_all, turn, acc, wg_buf, wd_buf, h_buf, part, sbuf, rbuf, zsend, zown, zrecv,
    tok_sem, wg_sem, wd_sem, tz_send, tz_recv, gz_send, gz_recv,
    tc_send, tc_recv, rc_send, rc_recv, rz_send, rz_recv,
):
    rows, depth = tok_hbm.shape
    quarter = depth // n_col
    local_experts, hid = wg_buf.shape[1], wg_buf.shape[3]
    chunks = wd_buf.shape[0]
    lanes = g_all.shape[1]
    total = tok_all.shape[0]
    bits = []
    while (1 << len(bits)) < n_col:
        bits.append(1 << len(bits))
    me = lax.axis_index("ep")
    col = lax.axis_index("col")

    def low(k):
        return k & -k if k else n_col

    def partner(bit):
        return col + bit - 2 * bit * lax.rem(lax.div(col, bit), 2)

    def piece(k):
        p = col
        for bit in bits:
            if k & bit:
                p = p + bit - 2 * bit * lax.rem(lax.div(col, bit), 2)
        return p

    def block(index):
        return pl.ds(pl.multiple_of(index * rows, rows), rows)

    def columns(k):
        return pl.ds(pl.multiple_of(piece(k) * quarter, 128), quarter)

    def wg_copy(k, e):
        return pltpu.make_async_copy(
            wg_hbm.at[e, columns(k)], wg_buf.at[k, e], wg_sem.at[k, e]
        )

    def wd_copy(j, k):
        at = pl.ds(pl.multiple_of(piece(k) * quarter + j * width, 128), width)
        return pltpu.make_async_copy(
            wd_hbm.at[:, :, at], wd_buf.at[j, k], wd_sem.at[j, k]
        )

    def wd_start(j):
        for k in range(n_col):
            wd_copy(j, k).start()

    def tok_z(d):
        return pltpu.make_async_remote_copy(
            src_ref=tok_hbm.at[:, columns(0)],
            dst_ref=tok_all.at[block(me), columns(0)],
            send_sem=tz_send.at[d], recv_sem=tz_recv.at[d],
            device_id={"ep": lax.rem(me + d, n_ep)}, device_id_type=MESH,
        )

    def gate_z(d):
        return pltpu.make_async_remote_copy(
            src_ref=g_all.at[block(me)], dst_ref=g_all.at[block(me)],
            send_sem=gz_send.at[d], recv_sem=gz_recv.at[d],
            device_id={"ep": lax.rem(me + d, n_ep)}, device_id_type=MESH,
        )

    def tok_c(d, k, bit):
        view = tok_all.at[block(lax.rem(me - d + n_ep, n_ep)), columns(k)]
        return pltpu.make_async_remote_copy(
            src_ref=view, dst_ref=view,
            send_sem=tc_send.at[d, k | bit], recv_sem=tc_recv.at[d, k | bit],
            device_id={"col": partner(bit)}, device_id_type=MESH,
        )

    def red_c(j, k):
        return pltpu.make_async_remote_copy(
            src_ref=sbuf.at[j, k - 1], dst_ref=rbuf.at[j, k - 1],
            send_sem=rc_send.at[j, k], recv_sem=rc_recv.at[j, k],
            device_id={"col": partner(low(k))}, device_id_type=MESH,
        )

    def red_z(j, d):
        return pltpu.make_async_remote_copy(
            src_ref=zsend.at[j, lax.rem(me + d, n_ep)], dst_ref=zrecv.at[j, d - 1],
            send_sem=rz_send.at[j, d], recv_sem=rz_recv.at[j, d],
            device_id={"ep": lax.rem(me + d, n_ep)}, device_id_type=MESH,
        )

    def each(lo, hi, body):
        def step(i, carry):
            body(i)
            return carry
        lax.fori_loop(lo, hi, step, 0)

    barrier = pltpu.get_barrier_semaphore()
    each(1, n_ep, lambda d: pl.semaphore_signal(
        barrier, inc=1, device_id={"ep": lax.rem(me + d, n_ep)}, device_id_type=MESH))
    for bit in bits:
        pl.semaphore_signal(
            barrier, inc=1, device_id={"col": partner(bit)}, device_id_type=MESH)

    own_copy = pltpu.make_async_copy(tok_hbm, tok_all.at[block(me)], tok_sem)
    own_copy.start()
    each(0, local_experts, lambda e: wg_copy(0, e).start())

    expert = lax.broadcasted_iota(jnp.int32, (lanes, rows), 0)
    dense = jnp.zeros((lanes, rows), jnp.float32)
    for k in range(routes_ref.shape[0]):
        dense = dense + jnp.where(
            routes_ref[k : k + 1, :] == expert, gates_ref[k : k + 1, :], 0.0)
    turn[...] = jnp.zeros_like(turn)
    turn[:, :rows] = dense
    g_all[block(me), :] = turn[...].T[:rows]

    pl.semaphore_wait(barrier, n_ep - 1 + len(bits))

    each(1, n_ep, lambda d: tok_z(d).start())
    each(1, n_ep, lambda d: gate_z(d).start())
    for k in range(1, n_col):
        each(0, local_experts, lambda e: wg_copy(k, e).start())
    each(0, min(AHEAD, chunks), wd_start)

    def up(k, e):
        wg_copy(k, e).wait()
        v = jnp.dot(tok_all[:, columns(k)], wg_buf[k, e], preferred_element_type=jnp.float32)
        if k:
            v = v + acc[e]
        if k < n_col - 1:
            acc[e] = v
            return
        mine = lax.broadcasted_iota(jnp.int32, (total, lanes), 1) == me * local_experts + e
        weight = jnp.sum(jnp.where(mine, g_all[...], 0.0), axis=1, keepdims=True)
        h = v / (1.0 + jnp.exp(-v))
        h_buf[:, pl.ds(pl.multiple_of(e * hid, 128), hid)] = (h * weight).astype(h_buf.dtype)

    for k in range(n_col):
        def arrived(d):
            if k:
                tok_c(d, k ^ low(k), low(k)).wait_recv()
            else:
                tok_z(d).wait_recv()
            for bit in reversed(bits):
                if bit < low(k):
                    tok_c(d, k, bit).start()

        each(1, n_ep, arrived)
        if k == 0:
            own_copy.wait()
        if k == n_col - 1:
            each(1, n_ep, lambda d: gate_z(d).wait_recv())
        each(0, local_experts, functools.partial(up, k))
        for j in range(AHEAD + k * chunks // n_col, AHEAD + (k + 1) * chunks // n_col):
            if j < chunks:
                wd_start(j)

    order = [k for k in range(n_col) if k & 1] + [k for k in range(n_col) if not k & 1]
    if n_col == 1:
        order = [0]

    def down(j):
        for k in order:
            wd_copy(j, k).wait()
            y = jnp.dot(
                h_buf[...], wd_buf[j, k].reshape(local_experts * hid, width),
                preferred_element_type=jnp.float32)
            if k & 1:
                sbuf[j, k - 1] = y.astype(sbuf.dtype)
                red_c(j, k).start()
            else:
                part[j, k // 2] = y

    def reduce_stage(j, bit):
        for k in reversed(range(0, n_col, 2 * bit)):
            red_c(j, k | bit).wait_recv()
            y = part[j, k // 2] + rbuf[j, (k | bit) - 1].astype(jnp.float32)
            if k and low(k) == 2 * bit:
                sbuf[j, k - 1] = y.astype(sbuf.dtype)
                red_c(j, k).start()
            elif k or 2 * bit < n_col:
                part[j, k // 2] = y
            else:
                finish(j, y)

    def finish(j, y):
        part[j, 0] = y
        zsend[j] = y.astype(zsend.dtype).reshape(n_ep, rows, width)
        zown[j] = part[j, 0, block(me), :]
        each(1, n_ep, lambda d: red_z(j, d).start())

    def step(t):
        @pl.when(t < chunks)
        def _():
            down(t)

        for i, bit in enumerate(bits):
            j = t - LAG * (i + 1)

            @pl.when((j >= 0) & (j < chunks))
            def _():
                reduce_stage(j, bit)

    each(0, chunks + LAG * len(bits), step)

    def last(j):
        def add(d, y):
            red_z(j, d).wait_recv()
            return y + zrecv[j, d - 1].astype(jnp.float32)

        y = lax.fori_loop(1, n_ep, add, zown[j])
        out_ref[:, pl.ds(pl.multiple_of(j * width, 128), width)] = y.astype(out_ref.dtype)

    each(0, chunks, last)

    def sent(d):
        tok_z(d).wait_send()
        gate_z(d).wait_send()
        for k in range(1, n_col):
            tok_c(d, k ^ low(k), low(k)).wait_send()

    each(1, n_ep, sent)

    def sent_chunk(j):
        for k in range(1, n_col):
            red_c(j, k).wait_send()
        each(1, n_ep, lambda d: red_z(j, d).wait_send())

    each(0, chunks, sent_chunk)


def on_device(tokens, routes, route_gates, gate_weight, down_weight):
    rows, depth = tokens.shape
    local_experts, _, hid = gate_weight.shape
    n_ep, n_col = lax.axis_size("ep"), lax.axis_size("col")
    quarter = depth // n_col
    width = 256 if quarter % 256 == 0 else 128
    chunks = quarter // width
    total = n_ep * rows
    lanes = -(-local_experts * n_ep // 128) * 128
    bf16, f32 = jnp.bfloat16, jnp.float32
    dma = pltpu.SemaphoreType.DMA
    vmem = pl.BlockSpec(memory_space=pltpu.VMEM)
    hbm = pl.BlockSpec(memory_space=pl.ANY)
    flops = 4 * total * depth * local_experts * hid
    return pl.pallas_call(
        functools.partial(kernel, n_ep, n_col, width),
        out_shape=jax.ShapeDtypeStruct((rows, quarter), tokens.dtype),
        in_specs=[hbm, vmem, vmem, hbm, hbm],
        out_specs=vmem,
        scratch_shapes=[
            pltpu.VMEM((total, depth), bf16),
            pltpu.VMEM((total, lanes), f32),
            pltpu.VMEM((lanes, 128), f32),
            pltpu.VMEM((local_experts, total, hid), f32),
            pltpu.VMEM((n_col, local_experts, quarter, hid), bf16),
            pltpu.VMEM((chunks, n_col, local_experts, hid, width), bf16),
            pltpu.VMEM((total, local_experts * hid), bf16),
            pltpu.VMEM((chunks, max(1, n_col // 2), total, width), f32),
            pltpu.VMEM((chunks, n_col - 1, total, width), bf16),
            pltpu.VMEM((chunks, n_col - 1, total, width), bf16),
            pltpu.VMEM((chunks, n_ep, rows, width), bf16),
            pltpu.VMEM((chunks, rows, width), f32),
            pltpu.VMEM((chunks, n_ep - 1, rows, width), bf16),
            dma,
            dma((n_col, local_experts)),
            dma((chunks, n_col)),
            dma((n_ep,)), dma((n_ep,)), dma((n_ep,)), dma((n_ep,)),
            dma((n_ep, n_col)), dma((n_ep, n_col)),
            dma((chunks, n_col)), dma((chunks, n_col)),
            dma((chunks, n_ep)), dma((chunks, n_ep)),
        ],
        compiler_params=pltpu.CompilerParams(
            collective_id=0, has_side_effects=True, vmem_limit_bytes=63 * 1024 * 1024
        ),
        cost_estimate=pl.CostEstimate(
            flops=flops, bytes_accessed=4 * local_experts * depth * hid, transcendentals=0
        ),
    )(tokens, routes.T, route_gates.T, gate_weight, down_weight)


def solution(mesh):
    in_specs = (
        P(("groups", "ep"), None),
        P(("groups", "ep"), None),
        P(("groups", "ep"), None),
        P("ep", None, "col"),
        P("ep", "col", None),
    )
    out_specs = P(("groups", "ep"), "col")
    return jax.shard_map(
        on_device, mesh=mesh, in_specs=in_specs, out_specs=out_specs, check_vma=False
    )
```

```python
import functools

import jax
import jax.numpy as jnp
from jax import lax
from jax.experimental import pallas as pl
from jax.experimental.pallas import tpu as pltpu
from jax.sharding import PartitionSpec as P

MESH = pl.DeviceIdType.MESH
AHEAD = 2
LAG = 4
BATCH = 8


def kernel(
    n_ep, n_col, width,
    tok_hbm, routes_ref, gates_ref, wg_hbm, wd_hbm, out_ref,
    tok_all, g_all, turn, acc, wg_buf, wd_buf, h_buf, part, sbuf, rbuf, zsend, zown, zrecv,
    tok_sem, wg_sem, wd_sem, tz_send, tz_recv, gz_send, gz_recv,
    tc_send, tc_recv, rc_send, rc_recv, rz_send, rz_recv,
):
    rows, depth = tok_hbm.shape
    quarter = depth // n_col
    local_experts, hid = wg_buf.shape[1], wg_buf.shape[3]
    chunks = wd_buf.shape[0]
    lanes = g_all.shape[1]
    total = tok_all.shape[0]
    bits = []
    while (1 << len(bits)) < n_col:
        bits.append(1 << len(bits))
    me = lax.axis_index("ep")
    col = lax.axis_index("col")

    def low(k):
        return k & -k if k else n_col

    def partner(bit):
        return col + bit - 2 * bit * lax.rem(lax.div(col, bit), 2)

    def piece(k):
        p = col
        for bit in bits:
            if k & bit:
                p = p + bit - 2 * bit * lax.rem(lax.div(col, bit), 2)
        return p

    def block(index):
        return pl.ds(pl.multiple_of(index * rows, rows), rows)

    def columns(k):
        return pl.ds(pl.multiple_of(piece(k) * quarter, 128), quarter)

    def wg_copy(k, e):
        return pltpu.make_async_copy(
            wg_hbm.at[e, columns(k)], wg_buf.at[k, e], wg_sem.at[k, e]
        )

    def wd_copy(j, k):
        at = pl.ds(pl.multiple_of(piece(k) * quarter + j * width, 128), width)
        return pltpu.make_async_copy(
            wd_hbm.at[:, :, at], wd_buf.at[j, k], wd_sem.at[j, k]
        )

    def wd_start(j):
        for k in range(n_col):
            wd_copy(j, k).start()

    def tok_z(d):
        return pltpu.make_async_remote_copy(
            src_ref=tok_hbm.at[:, columns(0)],
            dst_ref=tok_all.at[block(me), columns(0)],
            send_sem=tz_send.at[d], recv_sem=tz_recv.at[d],
            device_id={"ep": lax.rem(me + d, n_ep)}, device_id_type=MESH,
        )

    def gate_z(d):
        return pltpu.make_async_remote_copy(
            src_ref=g_all.at[block(me)], dst_ref=g_all.at[block(me)],
            send_sem=gz_send.at[d], recv_sem=gz_recv.at[d],
            device_id={"ep": lax.rem(me + d, n_ep)}, device_id_type=MESH,
        )

    def tok_c(d, k, bit):
        view = tok_all.at[block(lax.rem(me - d + n_ep, n_ep)), columns(k)]
        return pltpu.make_async_remote_copy(
            src_ref=view, dst_ref=view,
            send_sem=tc_send.at[d, k | bit], recv_sem=tc_recv.at[d, k | bit],
            device_id={"col": partner(bit)}, device_id_type=MESH,
        )

    def red_c(j, k):
        return pltpu.make_async_remote_copy(
            src_ref=sbuf.at[j, k - 1], dst_ref=rbuf.at[j, k - 1],
            send_sem=rc_send.at[j, k], recv_sem=rc_recv.at[j, k],
            device_id={"col": partner(low(k))}, device_id_type=MESH,
        )

    def red_z(j, d):
        return pltpu.make_async_remote_copy(
            src_ref=zsend.at[j, lax.rem(me + d, n_ep)], dst_ref=zrecv.at[j, d - 1],
            send_sem=rz_send.at[j, d], recv_sem=rz_recv.at[j, d],
            device_id={"ep": lax.rem(me + d, n_ep)}, device_id_type=MESH,
        )

    def each(lo, hi, body):
        def step(i, carry):
            body(i)
            return carry
        lax.fori_loop(lo, hi, step, 0)

    barrier = pltpu.get_barrier_semaphore()
    each(1, n_ep, lambda d: pl.semaphore_signal(
        barrier, inc=1, device_id={"ep": lax.rem(me + d, n_ep)}, device_id_type=MESH))
    for bit in bits:
        pl.semaphore_signal(
            barrier, inc=1, device_id={"col": partner(bit)}, device_id_type=MESH)

    own_copy = pltpu.make_async_copy(tok_hbm, tok_all.at[block(me)], tok_sem)
    own_copy.start()
    each(0, local_experts, lambda e: wg_copy(0, e).start())

    expert = lax.broadcasted_iota(jnp.int32, (lanes, rows), 0)
    dense = jnp.zeros((lanes, rows), jnp.float32)
    for k in range(routes_ref.shape[0]):
        dense = dense + jnp.where(
            routes_ref[k : k + 1, :] == expert, gates_ref[k : k + 1, :], 0.0)
    turn[...] = jnp.zeros_like(turn)
    turn[:, :rows] = dense
    g_all[block(me), :] = turn[...].T[:rows]

    pl.semaphore_wait(barrier, n_ep - 1 + len(bits))

    each(1, n_ep, lambda d: tok_z(d).start())
    each(1, n_ep, lambda d: gate_z(d).start())
    for k in range(1, n_col):
        each(0, local_experts, lambda e: wg_copy(k, e).start())
    each(0, min(AHEAD, chunks), wd_start)

    def up(k, e):
        v = jnp.dot(tok_all[:, columns(k)], wg_buf[k, e], preferred_element_type=jnp.float32)
        if k:
            v = v + acc[e]
        if k < n_col - 1:
            acc[e] = v
            return
        mine = lax.broadcasted_iota(jnp.int32, (total, lanes), 1) == me * local_experts + e
        weight = jnp.sum(jnp.where(mine, g_all[...], 0.0), axis=1, keepdims=True)
        h = v / (1.0 + jnp.exp(-v))
        h_buf[:, pl.ds(pl.multiple_of(e * hid, 128), hid)] = (h * weight).astype(h_buf.dtype)

    batch = BATCH if local_experts % BATCH == 0 else 1

    def up_batch(k, i):
        for m in range(batch):
            wg_copy(k, i * batch + m).wait()
        for m in range(batch):
            up(k, i * batch + m)

    for k in range(n_col):
        def arrived(d):
            if k:
                tok_c(d, k ^ low(k), low(k)).wait_recv()
            else:
                tok_z(d).wait_recv()
            for bit in reversed(bits):
                if bit < low(k):
                    tok_c(d, k, bit).start()

        each(1, n_ep, arrived)
        if k == 0:
            own_copy.wait()
        if k == n_col - 1:
            each(1, n_ep, lambda d: gate_z(d).wait_recv())
        each(0, local_experts // batch, functools.partial(up_batch, k))
        for j in range(AHEAD + k * chunks // n_col, AHEAD + (k + 1) * chunks // n_col):
            if j < chunks:
                wd_start(j)

    order = [k for k in range(n_col) if k & 1] + [k for k in range(n_col) if not k & 1]
    if n_col == 1:
        order = [0]

    def down(j):
        for k in order:
            wd_copy(j, k).wait()
        for k in order:
            y = jnp.dot(
                h_buf[...], wd_buf[j, k].reshape(local_experts * hid, width),
                preferred_element_type=jnp.float32)
            if k & 1:
                sbuf[j, k - 1] = y.astype(sbuf.dtype)
            else:
                part[j, k // 2] = y
            if k == n_col - 1:
                for odd in range(1, n_col, 2):
                    red_c(j, odd).start()

    def reduce_stage(j, bit):
        for k in reversed(range(0, n_col, 2 * bit)):
            red_c(j, k | bit).wait_recv()
            y = part[j, k // 2] + rbuf[j, (k | bit) - 1].astype(jnp.float32)
            if k and low(k) == 2 * bit:
                sbuf[j, k - 1] = y.astype(sbuf.dtype)
                red_c(j, k).start()
            elif k or 2 * bit < n_col:
                part[j, k // 2] = y
            else:
                finish(j, y)

    def finish(j, y):
        part[j, 0] = y
        zsend[j] = y.astype(zsend.dtype).reshape(n_ep, rows, width)
        zown[j] = part[j, 0, block(me), :]
        each(1, n_ep, lambda d: red_z(j, d).start())

    def step(t):
        @pl.when(t < chunks)
        def _():
            down(t)

        for i, bit in enumerate(bits):
            j = t - LAG * (i + 1)

            @pl.when((j >= 0) & (j < chunks))
            def _():
                reduce_stage(j, bit)

    each(0, chunks + LAG * len(bits), step)

    def last(j):
        def add(d, y):
            red_z(j, d).wait_recv()
            return y + zrecv[j, d - 1].astype(jnp.float32)

        y = lax.fori_loop(1, n_ep, add, zown[j])
        out_ref[:, pl.ds(pl.multiple_of(j * width, 128), width)] = y.astype(out_ref.dtype)

    each(0, chunks, last)

    def sent(d):
        tok_z(d).wait_send()
        gate_z(d).wait_send()
        for k in range(1, n_col):
            tok_c(d, k ^ low(k), low(k)).wait_send()

    each(1, n_ep, sent)

    def sent_chunk(j):
        for k in range(1, n_col):
            red_c(j, k).wait_send()
        each(1, n_ep, lambda d: red_z(j, d).wait_send())

    each(0, chunks, sent_chunk)


def on_device(tokens, routes, route_gates, gate_weight, down_weight):
    rows, depth = tokens.shape
    local_experts, _, hid = gate_weight.shape
    n_ep, n_col = lax.axis_size("ep"), lax.axis_size("col")
    quarter = depth // n_col
    width = 256 if quarter % 256 == 0 else 128
    chunks = quarter // width
    total = n_ep * rows
    lanes = -(-local_experts * n_ep // 128) * 128
    bf16, f32 = jnp.bfloat16, jnp.float32
    dma = pltpu.SemaphoreType.DMA
    vmem = pl.BlockSpec(memory_space=pltpu.VMEM)
    hbm = pl.BlockSpec(memory_space=pl.ANY)
    flops = 4 * total * depth * local_experts * hid
    return pl.pallas_call(
        functools.partial(kernel, n_ep, n_col, width),
        out_shape=jax.ShapeDtypeStruct((rows, quarter), tokens.dtype),
        in_specs=[hbm, vmem, vmem, hbm, hbm],
        out_specs=vmem,
        scratch_shapes=[
            pltpu.VMEM((total, depth), bf16),
            pltpu.VMEM((total, lanes), f32),
            pltpu.VMEM((lanes, 128), f32),
            pltpu.VMEM((local_experts, total, hid), f32),
            pltpu.VMEM((n_col, local_experts, quarter, hid), bf16),
            pltpu.VMEM((chunks, n_col, local_experts, hid, width), bf16),
            pltpu.VMEM((total, local_experts * hid), bf16),
            pltpu.VMEM((chunks, max(1, n_col // 2), total, width), f32),
            pltpu.VMEM((chunks, n_col - 1, total, width), bf16),
            pltpu.VMEM((chunks, n_col - 1, total, width), bf16),
            pltpu.VMEM((chunks, n_ep, rows, width), bf16),
            pltpu.VMEM((chunks, rows, width), f32),
            pltpu.VMEM((chunks, n_ep - 1, rows, width), bf16),
            dma,
            dma((n_col, local_experts)),
            dma((chunks, n_col)),
            dma((n_ep,)), dma((n_ep,)), dma((n_ep,)), dma((n_ep,)),
            dma((n_ep, n_col)), dma((n_ep, n_col)),
            dma((chunks, n_col)), dma((chunks, n_col)),
            dma((chunks, n_ep)), dma((chunks, n_ep)),
        ],
        compiler_params=pltpu.CompilerParams(
            collective_id=0, has_side_effects=True, vmem_limit_bytes=63 * 1024 * 1024
        ),
        cost_estimate=pl.CostEstimate(
            flops=flops, bytes_accessed=4 * local_experts * depth * hid, transcendentals=0
        ),
    )(tokens, routes.T, route_gates.T, gate_weight, down_weight)


def solution(mesh):
    in_specs = (
        P(("groups", "ep"), None),
        P(("groups", "ep"), None),
        P(("groups", "ep"), None),
        P("ep", None, "col"),
        P("ep", "col", None),
    )
    out_specs = P(("groups", "ep"), "col")
    return jax.shard_map(
        on_device, mesh=mesh, in_specs=in_specs, out_specs=out_specs, check_vma=False
    )
```

```python
import functools

import jax
import jax.numpy as jnp
from jax import lax
from jax.experimental import pallas as pl
from jax.experimental.pallas import tpu as pltpu
from jax.sharding import PartitionSpec as P

MESH = pl.DeviceIdType.MESH
AHEAD = 2
LAG = 4
BATCH = 8


def kernel(
    n_ep, n_col, width,
    tok_hbm, routes_ref, gates_ref, wg_hbm, wd_hbm, out_ref,
    tok_all, g_all, turn, acc, wg_buf, wd_buf, h_buf, part, sbuf, rbuf, zsend, zown, zrecv,
    tok_sem, wg_sem, wd_sem, tz_send, tz_recv, gz_send, gz_recv,
    tc_send, tc_recv, rc_send, rc_recv, rz_send, rz_recv,
):
    rows, depth = tok_hbm.shape
    quarter = depth // n_col
    local_experts, hid = wg_buf.shape[1], wg_buf.shape[3]
    chunks = wd_buf.shape[0]
    lanes = g_all.shape[1]
    total = tok_all.shape[0]
    bits = []
    while (1 << len(bits)) < n_col:
        bits.append(1 << len(bits))
    me = lax.axis_index("ep")
    col = lax.axis_index("col")

    def low(k):
        return k & -k if k else n_col

    def partner(bit):
        return col + bit - 2 * bit * lax.rem(lax.div(col, bit), 2)

    def piece(k):
        p = col
        for bit in bits:
            if k & bit:
                p = p + bit - 2 * bit * lax.rem(lax.div(col, bit), 2)
        return p

    def block(index):
        return pl.ds(pl.multiple_of(index * rows, rows), rows)

    def columns(k):
        return pl.ds(pl.multiple_of(piece(k) * quarter, 128), quarter)

    def wg_copy(k, e):
        return pltpu.make_async_copy(
            wg_hbm.at[e, columns(k)], wg_buf.at[k, e], wg_sem.at[k, e]
        )

    def wd_copy(j, k):
        at = pl.ds(pl.multiple_of(piece(k) * quarter + j * width, 128), width)
        return pltpu.make_async_copy(
            wd_hbm.at[:, :, at], wd_buf.at[j, k], wd_sem.at[j, k]
        )

    def wd_start(j):
        for k in range(n_col):
            wd_copy(j, k).start()

    def tok_z(d):
        return pltpu.make_async_remote_copy(
            src_ref=tok_hbm.at[:, columns(0)],
            dst_ref=tok_all.at[block(me), columns(0)],
            send_sem=tz_send.at[d], recv_sem=tz_recv.at[d],
            device_id={"ep": lax.rem(me + d, n_ep)}, device_id_type=MESH,
        )

    def gate_z(d):
        return pltpu.make_async_remote_copy(
            src_ref=g_all.at[block(me)], dst_ref=g_all.at[block(me)],
            send_sem=gz_send.at[d], recv_sem=gz_recv.at[d],
            device_id={"ep": lax.rem(me + d, n_ep)}, device_id_type=MESH,
        )

    def tok_c(d, k, bit):
        view = tok_all.at[block(lax.rem(me - d + n_ep, n_ep)), columns(k)]
        return pltpu.make_async_remote_copy(
            src_ref=view, dst_ref=view,
            send_sem=tc_send.at[d, k | bit], recv_sem=tc_recv.at[d, k | bit],
            device_id={"col": partner(bit)}, device_id_type=MESH,
        )

    def red_c(j, k):
        return pltpu.make_async_remote_copy(
            src_ref=sbuf.at[j, k - 1], dst_ref=rbuf.at[j, k - 1],
            send_sem=rc_send.at[j, k], recv_sem=rc_recv.at[j, k],
            device_id={"col": partner(low(k))}, device_id_type=MESH,
        )

    def red_z(j, d):
        return pltpu.make_async_remote_copy(
            src_ref=zsend.at[j, lax.rem(me + d, n_ep)], dst_ref=zrecv.at[j, d - 1],
            send_sem=rz_send.at[j, d], recv_sem=rz_recv.at[j, d],
            device_id={"ep": lax.rem(me + d, n_ep)}, device_id_type=MESH,
        )

    def each(lo, hi, body):
        def step(i, carry):
            body(i)
            return carry
        lax.fori_loop(lo, hi, step, 0)

    barrier = pltpu.get_barrier_semaphore()
    each(1, n_ep, lambda d: pl.semaphore_signal(
        barrier, inc=1, device_id={"ep": lax.rem(me + d, n_ep)}, device_id_type=MESH))
    for bit in bits:
        pl.semaphore_signal(
            barrier, inc=1, device_id={"col": partner(bit)}, device_id_type=MESH)

    own_copy = pltpu.make_async_copy(tok_hbm, tok_all.at[block(me)], tok_sem)
    own_copy.start()
    each(0, local_experts, lambda e: wg_copy(0, e).start())
    for k in range(1, n_col):
        each(0, local_experts, lambda e: wg_copy(k, e).start())

    expert = lax.broadcasted_iota(jnp.int32, (lanes, rows), 0)
    dense = jnp.zeros((lanes, rows), jnp.float32)
    for k in range(routes_ref.shape[0]):
        dense = dense + jnp.where(
            routes_ref[k : k + 1, :] == expert, gates_ref[k : k + 1, :], 0.0)
    turn[...] = jnp.zeros_like(turn)
    turn[:, :rows] = dense
    g_all[block(me), :] = turn[...].T[:rows]

    pl.semaphore_wait(barrier, n_ep - 1 + len(bits))

    each(1, n_ep, lambda d: tok_z(d).start())
    each(1, n_ep, lambda d: gate_z(d).start())
    each(0, min(AHEAD, chunks), wd_start)

    def up(k, e):
        v = jnp.dot(tok_all[:, columns(k)], wg_buf[k, e], preferred_element_type=jnp.float32)
        if k:
            v = v + acc[e]
        if k < n_col - 1:
            acc[e] = v
            return
        mine = lax.broadcasted_iota(jnp.int32, (total, lanes), 1) == me * local_experts + e
        weight = jnp.sum(jnp.where(mine, g_all[...], 0.0), axis=1, keepdims=True)
        h = v / (1.0 + jnp.exp(-v))
        h_buf[:, pl.ds(pl.multiple_of(e * hid, 128), hid)] = (h * weight).astype(h_buf.dtype)

    batch = BATCH if local_experts % BATCH == 0 else 1

    def up_batch(k, i):
        for m in range(batch):
            wg_copy(k, i * batch + m).wait()
        for m in range(batch):
            up(k, i * batch + m)

    for k in range(n_col):
        def arrived(d):
            if k:
                tok_c(d, k ^ low(k), low(k)).wait_recv()
            else:
                tok_z(d).wait_recv()
            for bit in reversed(bits):
                if bit < low(k):
                    tok_c(d, k, bit).start()

        each(1, n_ep, arrived)
        if k == 0:
            own_copy.wait()
        if k == n_col - 1:
            each(1, n_ep, lambda d: gate_z(d).wait_recv())
        each(0, local_experts // batch, functools.partial(up_batch, k))
        for j in range(AHEAD + k * chunks // n_col, AHEAD + (k + 1) * chunks // n_col):
            if j < chunks:
                wd_start(j)

    order = [k for k in range(n_col) if k & 1] + [k for k in range(n_col) if not k & 1]
    if n_col == 1:
        order = [0]

    def down(j):
        for k in order:
            wd_copy(j, k).wait()
        for k in order:
            y = jnp.dot(
                h_buf[...], wd_buf[j, k].reshape(local_experts * hid, width),
                preferred_element_type=jnp.float32)
            if k & 1:
                sbuf[j, k - 1] = y.astype(sbuf.dtype)
            else:
                part[j, k // 2] = y
            if k == n_col - 1:
                for odd in range(1, n_col, 2):
                    red_c(j, odd).start()

    def reduce_stage(j, bit):
        for k in reversed(range(0, n_col, 2 * bit)):
            red_c(j, k | bit).wait_recv()
            y = part[j, k // 2] + rbuf[j, (k | bit) - 1].astype(jnp.float32)
            if k and low(k) == 2 * bit:
                sbuf[j, k - 1] = y.astype(sbuf.dtype)
                red_c(j, k).start()
            elif k or 2 * bit < n_col:
                part[j, k // 2] = y
            else:
                finish(j, y)

    def finish(j, y):
        part[j, 0] = y
        zsend[j] = y.astype(zsend.dtype).reshape(n_ep, rows, width)
        zown[j] = part[j, 0, block(me), :]
        each(1, n_ep, lambda d: red_z(j, d).start())

    def step(t):
        @pl.when(t < chunks)
        def _():
            down(t)

        for i, bit in enumerate(bits):
            j = t - LAG * (i + 1)

            @pl.when((j >= 0) & (j < chunks))
            def _():
                reduce_stage(j, bit)

    each(0, chunks + LAG * len(bits), step)

    def last(j):
        def add(d, y):
            red_z(j, d).wait_recv()
            return y + zrecv[j, d - 1].astype(jnp.float32)

        y = lax.fori_loop(1, n_ep, add, zown[j])
        out_ref[:, pl.ds(pl.multiple_of(j * width, 128), width)] = y.astype(out_ref.dtype)

    each(0, chunks, last)

    def sent(d):
        tok_z(d).wait_send()
        gate_z(d).wait_send()
        for k in range(1, n_col):
            tok_c(d, k ^ low(k), low(k)).wait_send()

    each(1, n_ep, sent)

    def sent_chunk(j):
        for k in range(1, n_col):
            red_c(j, k).wait_send()
        each(1, n_ep, lambda d: red_z(j, d).wait_send())

    each(0, chunks, sent_chunk)


def on_device(tokens, routes, route_gates, gate_weight, down_weight):
    rows, depth = tokens.shape
    local_experts, _, hid = gate_weight.shape
    n_ep, n_col = lax.axis_size("ep"), lax.axis_size("col")
    quarter = depth // n_col
    width = 256 if quarter % 256 == 0 else 128
    chunks = quarter // width
    total = n_ep * rows
    lanes = -(-local_experts * n_ep // 128) * 128
    bf16, f32 = jnp.bfloat16, jnp.float32
    dma = pltpu.SemaphoreType.DMA
    vmem = pl.BlockSpec(memory_space=pltpu.VMEM)
    hbm = pl.BlockSpec(memory_space=pl.ANY)
    flops = 4 * total * depth * local_experts * hid
    return pl.pallas_call(
        functools.partial(kernel, n_ep, n_col, width),
        out_shape=jax.ShapeDtypeStruct((rows, quarter), tokens.dtype),
        in_specs=[hbm, vmem, vmem, hbm, hbm],
        out_specs=vmem,
        scratch_shapes=[
            pltpu.VMEM((total, depth), bf16),
            pltpu.VMEM((total, lanes), f32),
            pltpu.VMEM((lanes, 128), f32),
            pltpu.VMEM((local_experts, total, hid), f32),
            pltpu.VMEM((n_col, local_experts, quarter, hid), bf16),
            pltpu.VMEM((chunks, n_col, local_experts, hid, width), bf16),
            pltpu.VMEM((total, local_experts * hid), bf16),
            pltpu.VMEM((chunks, max(1, n_col // 2), total, width), f32),
            pltpu.VMEM((chunks, n_col - 1, total, width), bf16),
            pltpu.VMEM((chunks, n_col - 1, total, width), bf16),
            pltpu.VMEM((chunks, n_ep, rows, width), bf16),
            pltpu.VMEM((chunks, rows, width), f32),
            pltpu.VMEM((chunks, n_ep - 1, rows, width), bf16),
            dma,
            dma((n_col, local_experts)),
            dma((chunks, n_col)),
            dma((n_ep,)), dma((n_ep,)), dma((n_ep,)), dma((n_ep,)),
            dma((n_ep, n_col)), dma((n_ep, n_col)),
            dma((chunks, n_col)), dma((chunks, n_col)),
            dma((chunks, n_ep)), dma((chunks, n_ep)),
        ],
        compiler_params=pltpu.CompilerParams(
            collective_id=0, has_side_effects=True, vmem_limit_bytes=63 * 1024 * 1024
        ),
        cost_estimate=pl.CostEstimate(
            flops=flops, bytes_accessed=4 * local_experts * depth * hid, transcendentals=0
        ),
    )(tokens, routes.T, route_gates.T, gate_weight, down_weight)


def solution(mesh):
    in_specs = (
        P(("groups", "ep"), None),
        P(("groups", "ep"), None),
        P(("groups", "ep"), None),
        P("ep", None, "col"),
        P("ep", "col", None),
    )
    out_specs = P(("groups", "ep"), "col")
    return jax.shard_map(
        on_device, mesh=mesh, in_specs=in_specs, out_specs=out_specs, check_vma=False
    )
```
